512 devices in a mesh: dp: 32 (over z, core), ctx: 16 (over x, y).
Axes of the slice: x: 4, y: 4, z: 16, core: 2. Of those that a mesh axis runs over, the one named last changes fastest.
Arguments:
- tokens: bfloat16 [65536, 4096], P(('dp', 'ctx')), parts along dimension 0, may hold values from -6 to 6
- selected: int32 [8192], P('dp'), parts along dimension 0, may hold values from 0 to 2047, as said below
- norm_gain: bfloat16 [4096], replicated, may hold values from 0.25 to 1.75
- router: bfloat16 [4096], replicated, may hold values from -0.09375 to 0.09375
- w_query: bfloat16 [4096, 2048], P(None, 'ctx'), as said below
- w_key: bfloat16 [4096, 512], P(None, 'ctx'), as said below
- w_value: bfloat16 [4096, 512], P(None, 'ctx'), may hold values from -0.09375 to 0.09375
- w_out: bfloat16 [2048, 4096], P('ctx'), may hold values from -0.125 to 0.125
Outputs:
- layer_out: bfloat16 [65536, 4096], P(('dp', 'ctx')), parts along dimension 0
The draws below stay inside these ranges and needn't reach their ends.
There are 32 independent parts, one for each index of `dp`. The reference program is written for one: setup_inputs(seed, part) draws one part's arguments, and reference() takes and returns one part's arrays. A program takes and returns all parts, laid end to end along the dimension named above; an argument that names none is the same for every part. Nothing has to cross between parts.
Inputs may be any that keep to these rules, and one draw needn't show every extreme that they name: `selected`: strictly increasing; of each index's block of 128 positions at most 32 are listed, and one block has exactly 32. `w_query`: entries lie within six times 4096 to the power -0.5 of zero. `w_key`: entries lie within six times 4096 to the power -0.5 of zero.
All inputs are finite; a program needn't handle non-finite values.
Results may differ from the reference program's by a relative error of at most 0.0036.
Values may be sent and summed in bfloat16 or wider, within the bound.
No kernel may reach another device: no remote copies, remote signals or barrier semaphores. Data moves between devices by JAX's collectives and lax.ppermute only.
A program may use at most 64 MiB of HBM per device.

```python
import jax
import jax.numpy as jnp
from jax import lax

D = 4096
HS = 128
HQ = 16
KVH = 4
TOK_DEV = 128
TOKENS = 2048
SEL_DEV = 16
N_CTX = 16


def draw_tokens(key, part):
    key = jax.random.fold_in(key, 21)
    key_noise = jax.random.fold_in(key, 0)
    rows = jnp.clip(jax.random.normal(key_noise, (TOKENS, D), jnp.float32), -6.0, 6.0)
    return rows.astype(jnp.bfloat16)


def draw_w_query(key, part):
    key = jax.random.fold_in(key, 31)
    key_base = jax.random.fold_in(key, 0)
    spread = D ** (-0.5)
    weights = jnp.clip(jax.random.normal(key_base, (D, HQ * HS), jnp.float32), -6.0, 6.0) * spread
    return weights.astype(jnp.bfloat16)


def draw_w_key(key, part):
    key = jax.random.fold_in(key, 41)
    spread = D ** (-0.5)
    weights = jnp.clip(jax.random.normal(key, (D, KVH * HS), jnp.float32), -6.0, 6.0) * spread
    return weights.astype(jnp.bfloat16)


def draw_selected(key, part):
    key = jax.random.fold_in(key, 11)
    key_order, key_shift, key_rank, key_zero = jax.random.split(key, 4)
    paired = (N_CTX - 2) // 2
    shift = jax.random.randint(key_shift, (paired,), 0, SEL_DEV - 1)
    nonzero = jnp.concatenate([jnp.array([2 * SEL_DEV], jnp.int32), (SEL_DEV + shift).astype(jnp.int32), (SEL_DEV - shift).astype(jnp.int32)])
    nonzero = jax.random.permutation(key_order, nonzero)
    zero_at = 1 + jax.random.randint(key_zero, (), 0, N_CTX - 2)
    index = jnp.arange(N_CTX, dtype=jnp.int32)
    source = jnp.clip(index - (index > zero_at).astype(jnp.int32), 0, N_CTX - 2)
    counts = jnp.where(index == zero_at, 0, nonzero[source]).astype(jnp.int32)
    noise = jax.random.randint(key_rank, (N_CTX, TOK_DEV), 0, 65536) * TOK_DEV + jnp.arange(TOK_DEV, dtype=jnp.int32)[None, :]
    column = jnp.arange(TOK_DEV, dtype=jnp.int32)[None, :]
    noise = jnp.where(column == 0, -2, jnp.where(column == TOK_DEV - 1, -1, noise))
    ranking = jnp.argsort(jnp.argsort(noise, axis=1), axis=1)
    flags = (ranking < counts[:, None]).astype(jnp.int32).reshape(N_CTX * TOK_DEV)
    listed = jnp.argsort(1 - flags, stable=True)
    return listed[:N_CTX * SEL_DEV].astype(jnp.int32)


def block_scale(stream_key, shape, cuts, least, top_value):
    loudness, own = 1.0, jax.random.fold_in(stream_key, 6)
    for axis_at, shards_of in cuts:
        draws = jnp.exp(jax.random.uniform(jax.random.fold_in(own, axis_at), (shards_of,), jnp.float32, least / len(cuts), top_value / len(cuts)))
        loudness = loudness * jnp.repeat(draws, shape[axis_at] // shards_of).reshape([-1 if axis == axis_at else 1 for axis in range(len(shape))])
    return loudness


def scatter_about(stream_key, shape, scale, limit, cuts=(), kind=jnp.bfloat16):
    gain = block_scale(stream_key, shape, cuts, -0.22, 0.18) if cuts else 1.0
    drawn = jax.random.normal(stream_key, shape, jnp.float32) * scale * gain
    return jnp.minimum(jnp.maximum(drawn, -limit), limit).astype(kind)


def setup_inputs(seed: int = 0, part: int = 0) -> dict:
    key_list = jax.random.split(jax.random.key(seed), 9)
    part_splits = jax.random.split(jax.random.fold_in(key_list[8], part), 9)
    return {
        "tokens": draw_tokens(jax.random.fold_in(jax.random.fold_in(key_list[8], part), 71), part),
        "selected": draw_selected(jax.random.fold_in(jax.random.fold_in(key_list[8], part), 71), part),
        "norm_gain": jnp.clip(1.0 + 0.15 * jax.random.normal(key_list[2], (D,), jnp.float32), 0.25, 1.75).astype(jnp.bfloat16),
        "router": scatter_about(key_list[3], (D,), D ** -0.5, 0.09375),
        "w_query": draw_w_query(jax.random.fold_in(key_list[8], 71), part),
        "w_key": draw_w_key(jax.random.fold_in(key_list[8], 71), part),
        "w_value": scatter_about(key_list[6], (D, KVH * HS), D ** -0.5, 0.09375, ((1, 16),)),
        "w_out": scatter_about(key_list[7], (HQ * HS, D), (HQ * HS) ** -0.5, 0.125, ((0, 16),)),
    }


def rotary(values, positions, offset):
    width = values.shape[1]
    column = offset + jnp.arange(width)
    pair = (column % HS // 2).astype(jnp.float32)
    inverse = jnp.exp(-(2.0 * pair / HS) * jnp.log(10000.0))
    angle = positions.astype(jnp.float32)[:, None] * inverse[None, :]
    cosine = jnp.cos(angle).reshape(values.shape[0], width // 2, 2)[:, :, 0]
    sine = jnp.sin(angle).reshape(values.shape[0], width // 2, 2)[:, :, 0]
    paired = values.reshape(values.shape[0], width // 2, 2)
    first = paired[:, :, 0]
    second = paired[:, :, 1]
    turned = jnp.stack([first * cosine - second * sine, first * sine + second * cosine], axis=2)
    return turned.reshape(values.shape[0], width)

def headwise(matrix):
    count = matrix.shape[0]
    return matrix.reshape(count, HS, KVH).transpose(0, 2, 1).reshape(count, KVH * HS)

def reference(tokens, selected, norm_gain, router, w_query, w_key, w_value, w_out):
    routed = tokens[selected]
    wide = routed.astype(jnp.float32)
    scale = jax.lax.rsqrt(lax.optimization_barrier(jnp.mean(wide * wide, axis=1, keepdims=True)) + 1e-05)
    normed = (wide * scale * norm_gain.astype(jnp.float32)[None, :]).astype(jnp.bfloat16)
    query = rotary(jnp.dot(normed, w_query, preferred_element_type=jnp.float32), selected, 0).astype(jnp.bfloat16)
    keys = rotary(headwise(jnp.dot(normed, w_key, preferred_element_type=jnp.float32)), selected, 0).astype(jnp.bfloat16)
    values = headwise(jnp.dot(normed, w_value, preferred_element_type=jnp.float32)).astype(jnp.bfloat16)
    count = routed.shape[0]
    grouped = HQ // KVH
    query_h = query.reshape(count, HQ, HS).astype(jnp.float32)
    keys_h = jnp.repeat(keys.reshape(count, KVH, HS), grouped, axis=1).astype(jnp.float32)
    values_h = jnp.repeat(values.reshape(count, KVH, HS), grouped, axis=1).astype(jnp.float32)
    scores = jnp.einsum('qhd,khd->hqk', query_h, keys_h) / jnp.sqrt(jnp.float32(HS))
    causal = jnp.arange(count)[:, None] >= jnp.arange(count)[None, :]
    scores = jnp.where(causal[None], scores, jnp.float32(-1e+30))
    top = lax.optimization_barrier(jnp.max(scores, axis=2, keepdims=True))
    weights = jnp.exp(scores - top)
    probs = (weights / lax.optimization_barrier(jnp.sum(weights, axis=2, keepdims=True))).astype(jnp.bfloat16)
    attended = jnp.einsum('hqk,khd->qhd', probs.astype(jnp.float32), values_h).astype(jnp.bfloat16)
    flat = attended.reshape(count, HQ * HS)
    per_group = HQ * HS // N_CTX
    update = jnp.zeros((count, w_out.shape[1]), jnp.float32)
    for group in range(N_CTX):
        partial_sum = jnp.dot(flat[:, group * per_group:(group + 1) * per_group], w_out[group * per_group:(group + 1) * per_group], preferred_element_type=jnp.float32).astype(jnp.bfloat16)
        partial_sum = lax.optimization_barrier(partial_sum)
        update = update + partial_sum.astype(jnp.float32)
    gate = jax.nn.sigmoid(jnp.dot(routed, router, preferred_element_type=jnp.float32))
    fresh = (wide + gate[:, None] * update).astype(jnp.bfloat16)
    return tokens.at[selected].set(fresh)
```

```python
import jax
import jax.numpy as jnp
from jax import lax
from jax.experimental import pallas as pl
from jax.experimental.pallas import tpu as pltpu
from jax.sharding import PartitionSpec as P

HS = 128
HQ = 16
KVH = 4
CAP = 32
N = 16
TOK = 128
SEL = 256
D = 4096
SL = D // N
BF = jnp.bfloat16
F32 = jnp.float32
NT = (((1,), (1,)), ((), ()))
CHUNK = SEL + SEL // 2


def one_hot(mask):
    return jnp.where(mask, 1.0, 0.0).astype(BF)


def slots(sel, me):
    base = me * TOK
    first = jnp.sum(jnp.where(sel < base, 1.0, 0.0), axis=1, keepdims=True).astype(jnp.int32)
    mine = (sel >= base) & (sel < base + TOK)
    rank = lax.broadcasted_iota(jnp.int32, (CAP, SEL), 1)
    slot = lax.broadcasted_iota(jnp.int32, (CAP, SEL), 0)
    by_slot = one_hot((rank - first == slot) & mine)
    token = lax.broadcasted_iota(jnp.int32, (TOK, SEL), 0)
    by_token = one_hot(token + base == sel)
    return by_slot, by_token


def pack_kernel(sel_ref, tok_ref, gain_ref, router_ref, wout_ref, send_ref, raw_ref, gate_ref):
    by_slot, by_token = slots(sel_ref[...], lax.axis_index("ctx"))
    pick = lax.dot_general(by_slot, by_token, NT, preferred_element_type=F32).astype(BF)
    raw = jnp.dot(pick, tok_ref[...], preferred_element_type=F32)
    raw_ref[...] = raw.astype(BF)
    scale = lax.rsqrt(jnp.mean(raw * raw, axis=1, keepdims=True) + 1e-05)
    normed = (raw * scale * gain_ref[...].astype(F32)).astype(BF)
    logit = jnp.sum(raw * router_ref[...].astype(F32), axis=1, keepdims=True)
    gate_ref[...] = jnp.broadcast_to(1.0 / (1.0 + jnp.exp(-logit)), (CAP, 128))
    for c in range(N):
        send_ref[c, :CAP, :] = normed[:, c * SL : (c + 1) * SL]
        send_ref[c, CAP:, :] = wout_ref[:, c * SL : (c + 1) * SL]


def compact_kernel(sel_row_ref, sel_col_ref, recv_ref, out_ref):
    sel_row, sel_col = sel_row_ref[...], sel_col_ref[...]
    owner = sel_col >> 7
    first = jnp.sum(jnp.where(sel_row < owner * TOK, 1.0, 0.0), axis=1, keepdims=True).astype(jnp.int32)
    place = owner * CAP + lax.broadcasted_iota(jnp.int32, (SEL, 1), 0) - first
    pick = one_hot(lax.broadcasted_iota(jnp.int32, (SEL, N * CAP), 1) == place)
    rows = recv_ref[:, :CAP, :].reshape(N * CAP, SL)
    dense = jnp.dot(pick, rows, preferred_element_type=F32).astype(BF)
    for d in range(N):
        out_ref[d] = dense


def qkv_kernel(x_ref, w_ref, cos_ref, sin_ref, out_ref):
    acc = jnp.zeros((SEL, 256), F32)
    for f in range(N):
        acc += jnp.dot(x_ref[f], w_ref[f * SL : (f + 1) * SL, :], preferred_element_type=F32)
    lane = lax.broadcasted_iota(jnp.int32, (SEL, 128), 1)
    q, kv = acc[:, :128], acc[:, 128:]
    q_mate = jnp.where(lane % 2 == 0, pltpu.roll(q, 127, 1), pltpu.roll(q, 1, 1))
    q = (q * cos_ref[:, :128] + q_mate * sin_ref[:, :128]).astype(BF)
    kv_mate = jnp.where(lane % 8 < 4, pltpu.roll(kv, 124, 1), pltpu.roll(kv, 4, 1))
    kv = (kv * cos_ref[:, 128:] + kv_mate * sin_ref[:, 128:]).astype(BF)
    to = lax.broadcasted_iota(jnp.int32, (64, 128), 0)
    frm = lax.broadcasted_iota(jnp.int32, (64, 128), 1)
    order = one_hot(frm == ((to >> 3) & 1) * 32 + (to & 7) * 4 + (to >> 4))
    turned = lax.dot_general(order, kv, NT, preferred_element_type=F32).astype(BF)
    for d in range(N):
        out_ref[d, :SEL, :] = q
        out_ref[d, SEL : SEL + 64, :] = turned[:, :128]
        out_ref[d, SEL + 64 :, :] = turned[:, 128:]


def attend_kernel(sel_row_ref, sel_col_ref, recv_ref, wout_ref, out_ref):
    left = recv_ref[:, SEL : SEL + 64, :].astype(F32).reshape(N, KVH, 2, 8, 128)
    right = recv_ref[:, SEL + 64 :, :].astype(F32).reshape(N, KVH, 2, 8, 128)
    row = lax.broadcasted_iota(jnp.int32, (SEL, SEL), 0)
    col = lax.broadcasted_iota(jnp.int32, (SEL, SEL), 1)
    causal = row >= col
    acc = jnp.zeros((SEL, SL), F32)
    for g in range(KVH):
        keys, values = [
            jnp.concatenate([half[:, g, i].reshape(HS, 128) for half in (left, right)], axis=1).astype(BF)
            for i in range(2)
        ]
        for h in range(g * HQ // KVH, (g + 1) * HQ // KVH):
            scores = jnp.dot(recv_ref[h, :SEL, :], keys, preferred_element_type=F32) * (HS**-0.5)
            scores = jnp.where(causal, scores, -1e30)
            weights = jnp.exp(scores - jnp.max(scores, axis=1, keepdims=True))
            probs = (weights / jnp.sum(weights, axis=1, keepdims=True)).astype(BF)
            mixed = lax.dot_general(probs, values, NT, preferred_element_type=F32).astype(BF)
            acc += jnp.dot(mixed, wout_ref[h, CAP:, :], preferred_element_type=F32)
    sel_row, sel_col = sel_row_ref[...], sel_col_ref[...]
    owner = sel_row >> 7
    first = jnp.sum(jnp.where(sel_col < owner * TOK, 1.0, 0.0), axis=0, keepdims=True).astype(jnp.int32)
    place = owner * CAP + lax.broadcasted_iota(jnp.int32, (1, SEL), 1) - first
    put = one_hot(lax.broadcasted_iota(jnp.int32, (N * CAP, SEL), 0) == place)
    sent = jnp.dot(put, acc.astype(BF), preferred_element_type=F32).astype(BF)
    out_ref[...] = sent.reshape(N, CAP, SL)


def finish_kernel(sel_ref, tok_ref, raw_ref, gate_ref, recv_ref, out_ref):
    by_slot, by_token = slots(sel_ref[...], lax.axis_index("ctx"))
    put = lax.dot_general(by_token, by_slot, NT, preferred_element_type=F32).astype(BF)
    live = jnp.sum(by_token.astype(F32), axis=1, keepdims=True) > 0.5
    gate = gate_ref[:, :1]
    for c in range(N):
        part = slice(c * SL, (c + 1) * SL)
        fresh = (raw_ref[:, part].astype(F32) + gate * recv_ref[c].astype(F32)).astype(BF)
        placed = jnp.dot(put, fresh, preferred_element_type=F32).astype(BF)
        out_ref[:, part] = jnp.where(live, placed, tok_ref[:, part])


def call(kernel, shapes, n_in, flops, moved, name):
    return pl.pallas_call(
        kernel,
        out_shape=shapes,
        in_specs=[pl.BlockSpec(memory_space=pltpu.VMEM)] * n_in,
        out_specs=jax.tree.map(lambda _: pl.BlockSpec(memory_space=pltpu.VMEM), shapes),
        compiler_params=pltpu.CompilerParams(vmem_limit_bytes=40 * 1024 * 1024),
        cost_estimate=pl.CostEstimate(flops=flops, bytes_accessed=moved, transcendentals=0),
        name=name,
    )


def on_device(tokens, selected, norm_gain, router, w_query, w_key, w_value, w_out):
    me = lax.axis_index("ctx")
    shape = jax.ShapeDtypeStruct
    sel_row, sel_col = selected.reshape(1, SEL), selected.reshape(SEL, 1)
    send, raw, gate = call(
        pack_kernel,
        (shape((N, CAP + TOK, SL), BF), shape((CAP, D), BF), shape((CAP, 128), F32)),
        5, 2 * CAP * TOK * D, 4 << 20, "pack",
    )(sel_row, tokens, norm_gain.reshape(1, D), router.reshape(1, D), w_out)
    got = lax.all_to_all(send, "ctx", 0, 0, tiled=True)
    weights = jnp.concatenate([w_query, w_key, w_value, jnp.zeros((D, 64), BF)], axis=1)
    lane = jnp.arange(256)
    component = jnp.where(lane < HS, lane, me * 8 + (lane - HS) // 4)
    pair = (component // 2).astype(F32)
    inverse = jnp.exp(-(2.0 * pair / HS) * jnp.log(10000.0))
    inverse = jnp.where(lane < HS + 32, inverse, 0.0)
    angle = selected.astype(F32)[:, None] * inverse[None, :]
    cosine = jnp.cos(angle)
    sine = jnp.sin(angle) * jnp.where(component % 2 == 0, -1.0, 1.0)[None, :]
    copies = call(compact_kernel, shape((N, SEL, SL), BF), 3, 2 * SEL * 512 * SL, 4 << 20, "compact")(
        sel_row, sel_col, got
    )
    rows = lax.all_to_all(copies, "ctx", 0, 0, tiled=True)
    qkv = call(qkv_kernel, shape((N, CHUNK, HS), BF), 4, 2 * SEL * D * 256, 6 << 20, "qkv")(
        rows, weights, cosine, sine
    )
    heads = lax.all_to_all(qkv, "ctx", 0, 0, tiled=True)
    update = call(attend_kernel, shape((N, CAP, SL), BF), 4, 2 * 16 * 3 * 256 * 256 * 128, 4 << 20, "attend")(
        sel_row, sel_col, heads, got
    )
    back = lax.all_to_all(update, "ctx", 0, 0, tiled=True)
    return call(finish_kernel, shape((TOK, D), BF), 5, 2 * TOK * CAP * D, 4 << 20, "finish")(
        sel_row, tokens, raw, gate, back
    )


def solution(mesh):
    placed = (
        P(("dp", "ctx"), None),
        P("dp"),
        P(),
        P(),
        P(None, "ctx"),
        P(None, "ctx"),
        P(None, "ctx"),
        P("ctx", None),
    )
    return jax.shard_map(
        on_device, mesh=mesh, in_specs=placed, out_specs=P(("dp", "ctx"), None), check_vma=False
    )
```

```python
import jax
import jax.numpy as jnp
from jax import lax
from jax.experimental import pallas as pl
from jax.experimental.pallas import tpu as pltpu
from jax.sharding import Mesh
from jax.sharding import PartitionSpec as P

HS = 128
HQ = 16
KVH = 4
CAP = 32
N = 16
TOK = 128
SEL = 256
D = 4096
SL = D // N
NZ = 16
BF = jnp.bfloat16
F32 = jnp.float32
NT = (((1,), (1,)), ((), ()))
CHUNK = SEL + SEL // 2
PIECE = 16
VMEM = pltpu.VMEM


def one_hot(mask):
    return jnp.where(mask, 1.0, 0.0).astype(BF)


def slots(sel, me):
    base = me * TOK
    first = jnp.sum(jnp.where(sel < base, 1.0, 0.0), axis=1, keepdims=True).astype(jnp.int32)
    mine = (sel >= base) & (sel < base + TOK)
    rank = lax.broadcasted_iota(jnp.int32, (CAP, SEL), 1)
    slot = lax.broadcasted_iota(jnp.int32, (CAP, SEL), 0)
    by_slot = one_hot((rank - first == slot) & mine)
    token = lax.broadcasted_iota(jnp.int32, (TOK, SEL), 0)
    by_token = one_hot(token + base == sel)
    return by_slot, by_token


def column(row):
    same = lax.broadcasted_iota(jnp.int32, (SEL, SEL), 0) == lax.broadcasted_iota(jnp.int32, (SEL, SEL), 1)
    return jnp.sum(jnp.where(same, row.astype(F32), 0.0), axis=1, keepdims=True).astype(jnp.int32)


def pack_kernel(sel_ref, tok_hbm, gain_ref, wout_hbm, send_ref, tok_ref, wout_ref, sems):
    z, me = lax.axis_index("z"), lax.axis_index("ctx")
    parts = 4
    height = TOK // parts
    loads = [
        pltpu.make_async_copy(
            tok_hbm.at[pl.ds(i * height, height)], tok_ref.at[pl.ds(i * height, height)], sems.at[i]
        )
        for i in range(parts)
    ]
    loads.append(
        pltpu.make_async_copy(
            wout_hbm.at[pl.ds(pl.multiple_of((z // 2) * PIECE, PIECE), PIECE)], wout_ref, sems.at[parts]
        )
    )
    for load in loads:
        load.start()
    by_slot, by_token = slots(sel_ref[...], me)
    pick = lax.dot_general(by_slot, by_token, NT, preferred_element_type=F32).astype(BF)
    for load in loads:
        load.wait()
    raw = jnp.dot(pick, tok_ref[...], preferred_element_type=F32)
    scale = lax.rsqrt(jnp.mean(raw * raw, axis=1, keepdims=True) + 1e-05)
    normed = (raw * scale * gain_ref[...].reshape(1, D).astype(F32)).astype(BF)
    right = z % 2 == 1
    for c in range(N):
        send_ref[c, :CAP, :] = normed[:, c * SL : c * SL + 128]
        send_ref[c, CAP : 2 * CAP, :] = normed[:, c * SL + 128 : (c + 1) * SL]
        send_ref[c, 2 * CAP :, :] = jnp.where(
            right, wout_ref[:, c * SL + 128 : (c + 1) * SL], wout_ref[:, c * SL : c * SL + 128]
        )


def compact_kernel(sel_ref, recv_ref, out_ref, piece_ref):
    sel_row = sel_ref[...]
    owner = column(sel_row) >> 7
    first = jnp.sum(jnp.where(sel_row < owner * TOK, 1.0, 0.0), axis=1, keepdims=True).astype(jnp.int32)
    place = owner * CAP + lax.broadcasted_iota(jnp.int32, (SEL, 1), 0) - first
    pick = one_hot(lax.broadcasted_iota(jnp.int32, (SEL, N * CAP), 1) == place)
    left = jnp.dot(pick, recv_ref[:, :CAP, :].reshape(N * CAP, 128), preferred_element_type=F32)
    right = jnp.dot(pick, recv_ref[:, CAP : 2 * CAP, :].reshape(N * CAP, 128), preferred_element_type=F32)
    dense = jnp.concatenate([left, right], axis=1).astype(BF)
    for d in range(N):
        out_ref[d] = dense
        piece_ref[d * PIECE : (d + 1) * PIECE, :] = recv_ref[d, 2 * CAP :, :]


def qkv_kernel(x_ref, wq_ref, wk_ref, wv_ref, qcos_ref, qsin_ref, kcos_ref, ksin_ref, out_ref):
    q = jnp.zeros((SEL, HS), F32)
    kv = jnp.zeros((SEL, 64), F32)
    for f in range(N):
        part = slice(f * SL, (f + 1) * SL)
        q += jnp.dot(x_ref[f], wq_ref[part, :], preferred_element_type=F32)
        both = jnp.concatenate([wk_ref[:, part], wv_ref[:, part]], axis=0)
        kv += lax.dot_general(x_ref[f], both, NT, preferred_element_type=F32)
    lane = lax.broadcasted_iota(jnp.int32, (SEL, 128), 1)
    q_mate = jnp.where(lane % 2 == 0, pltpu.roll(q, 127, 1), pltpu.roll(q, 1, 1))
    q = (q * qcos_ref[...] + q_mate * qsin_ref[...]).astype(BF)
    kv = jnp.concatenate([kv, kv], axis=1)
    kv_mate = jnp.where(lane % 8 < 4, pltpu.roll(kv, 124, 1), pltpu.roll(kv, 4, 1))
    kv = (kv * kcos_ref[...] + kv_mate * ksin_ref[...]).astype(BF)
    to = lax.broadcasted_iota(jnp.int32, (64, 128), 0)
    frm = lax.broadcasted_iota(jnp.int32, (64, 128), 1)
    order = one_hot(frm == ((to >> 3) & 1) * 32 + (to & 7) * 4 + (to >> 4))
    turned = lax.dot_general(order, kv, NT, preferred_element_type=F32).astype(BF)
    for d in range(N):
        out_ref[d, :SEL, :] = q
        out_ref[d, SEL : SEL + 64, :] = turned[:, :128]
        out_ref[d, SEL + 64 :, :] = turned[:, 128:]


def attend_kernel(sel_ref, recv_ref, wout_hbm, out_ref, wout_ref, mixed_ref, sems):
    parts = 4
    height = NZ * N * PIECE // parts
    loads = [
        pltpu.make_async_copy(
            wout_hbm.at[pl.ds(i * height, height)], wout_ref.at[pl.ds(i * height, height)], sems.at[i]
        )
        for i in range(parts)
    ]
    for load in loads:
        load.start()
    half = SEL // 2
    left = recv_ref[:, SEL : SEL + 64, :].astype(F32).reshape(N, KVH, 2, 8, half)
    right = recv_ref[:, SEL + 64 :, :].astype(F32).reshape(N, KVH, 2, 8, half)
    causal = lax.broadcasted_iota(jnp.int32, (half, half), 0) >= lax.broadcasted_iota(jnp.int32, (half, half), 1)

    def mix(scores, values):
        top = jnp.max(scores, axis=1, keepdims=True)
        weights = jnp.exp((scores - top) * (HS**-0.5))
        total = jnp.sum(weights, axis=1, keepdims=True)
        product = lax.dot_general(weights.astype(BF), values, NT, preferred_element_type=F32)
        return (product / total).astype(BF)

    for g in range(KVH):
        k_l, v_l = [left[:, g, i].reshape(HS, half).astype(BF) for i in range(2)]
        k_r, v_r = [right[:, g, i].reshape(HS, half).astype(BF) for i in range(2)]
        values = jnp.concatenate([v_l, v_r], axis=1)
        for h in range(g * HQ // KVH, (g + 1) * HQ // KVH):
            here = slice(h * HS, (h + 1) * HS)
            scores = jnp.dot(recv_ref[h, :SEL, :], k_l, preferred_element_type=F32)
            tail = jnp.dot(recv_ref[h, half:SEL, :], k_r, preferred_element_type=F32)
            upper = jnp.where(causal, scores[:half], -1e30)
            lower = jnp.concatenate([scores[half:], jnp.where(causal, tail, -1e30)], axis=1)
            mixed_ref[:half, here] = mix(upper, v_l)
            mixed_ref[half:, here] = mix(lower, values)
    for load in loads:
        load.wait()
    update = jnp.zeros((SEL, SL), F32)
    for h in range(HQ):
        rows = [
            jnp.concatenate(
                [wout_ref[pl.ds(((2 * b + s) * N + h) * PIECE, PIECE), :] for s in range(2)], axis=1
            )
            for b in range(HS // PIECE)
        ]
        update += jnp.dot(
            mixed_ref[:, h * HS : (h + 1) * HS], jnp.concatenate(rows, axis=0), preferred_element_type=F32
        )
    sel_row = sel_ref[...]
    owner = sel_row >> 7
    first = jnp.sum(
        jnp.where(column(sel_row) < owner * TOK, 1.0, 0.0), axis=0, keepdims=True
    ).astype(jnp.int32)
    place = owner * CAP + lax.broadcasted_iota(jnp.int32, (1, SEL), 1) - first
    put = one_hot(lax.broadcasted_iota(jnp.int32, (N * CAP, SEL), 0) == place)
    sent = jnp.dot(put, update.astype(BF), preferred_element_type=F32).astype(BF)
    out_ref[...] = sent.reshape(N, CAP, SL)


def finish_kernel(sel_ref, tok_ref, router_ref, recv_ref, out_ref):
    by_slot, by_token = slots(sel_ref[...], lax.axis_index("ctx"))
    put = lax.dot_general(by_token, by_slot, NT, preferred_element_type=F32).astype(BF)
    live = jnp.sum(by_token.astype(F32), axis=1, keepdims=True) > 0.5
    router = router_ref[...].reshape(1, D).astype(F32)
    logit = jnp.sum(tok_ref[...].astype(F32) * router, axis=1, keepdims=True)
    gate = 1.0 / (1.0 + jnp.exp(-logit))
    for c in range(N):
        part = slice(c * SL, (c + 1) * SL)
        placed = jnp.dot(put, recv_ref[c], preferred_element_type=F32)
        old = tok_ref[:, part]
        fresh = (old.astype(F32) + gate * placed).astype(BF)
        out_ref[:, part] = jnp.where(live, fresh, old)


def call(kernel, name, shapes, in_hbm, flops, moved, scratch=()):
    return pl.pallas_call(
        kernel,
        out_shape=shapes,
        in_specs=[pl.BlockSpec(memory_space=pl.ANY if hbm else VMEM) for hbm in in_hbm],
        out_specs=jax.tree.map(lambda _: pl.BlockSpec(memory_space=VMEM), shapes),
        scratch_shapes=scratch,
        compiler_params=pltpu.CompilerParams(vmem_limit_bytes=40 * 1024 * 1024),
        cost_estimate=pl.CostEstimate(flops=flops, bytes_accessed=moved, transcendentals=0),
        name=name,
    )


def on_device(tokens, selected, norm_gain, router, w_query, w_key, w_value, w_out):
    me = lax.axis_index("ctx")
    shape = jax.ShapeDtypeStruct
    sel = selected.reshape(1, SEL)
    lane = jnp.arange(HS)
    position = selected.astype(F32)[:, None]

    def turn(component, used):
        pair = (component // 2).astype(F32)
        inverse = jnp.exp(-(2.0 * pair / HS) * jnp.log(10000.0))
        angle = position * jnp.where(used, inverse, 0.0)[None, :]
        return jnp.cos(angle), jnp.sin(angle) * jnp.where(component % 2 == 0, -1.0, 1.0)[None, :]

    q_cos, q_sin = turn(lane, lane < HS)
    k_cos, k_sin = turn(me * 8 + lane // 4, lane < 32)
    send = call(
        pack_kernel, "pack", shape((N, 2 * CAP + PIECE, 128), BF), (0, 1, 0, 1), 2 * CAP * TOK * D, 2 << 20,
        [VMEM((TOK, D), BF), VMEM((PIECE, D), BF), pltpu.SemaphoreType.DMA((5,))],
    )(sel, tokens, norm_gain, w_out)
    got = lax.all_to_all(send, "ctx", 0, 0, tiled=True)
    copies, piece = call(
        compact_kernel, "compact", (shape((N, SEL, SL), BF), shape((N * PIECE, 128), BF)), (0, 0),
        2 * SEL * 512 * SL, 3 << 20,
    )(sel, got)
    w_slice = lax.all_gather(piece, "z", axis=0, tiled=True)
    rows = lax.all_to_all(copies, "ctx", 0, 0, tiled=True)
    qkv = call(qkv_kernel, "qkv", shape((N, CHUNK, HS), BF), (0,) * 8, 2 * SEL * D * 256, 6 << 20)(
        rows, w_query, w_key.T, w_value.T, q_cos, q_sin, k_cos, k_sin
    )
    heads = lax.all_to_all(qkv, "ctx", 0, 0, tiled=True)
    update = call(
        attend_kernel, "attend", shape((N, CAP, SL), BF), (0, 0, 1), 2 * 16 * 3 * 256 * 256 * 128, 4 << 20,
        [VMEM((NZ * N * PIECE, 128), BF), VMEM((SEL, HQ * HS), BF), pltpu.SemaphoreType.DMA((4,))],
    )(sel, heads, w_slice)
    back = lax.all_to_all(update, "ctx", 0, 0, tiled=True)
    return call(finish_kernel, "finish", shape((TOK, D), BF), (0,) * 4, 2 * TOK * CAP * D, 4 << 20)(
        sel, tokens, router, back
    )


def solution(mesh):
    split = Mesh(mesh.devices.reshape(NZ, mesh.shape["dp"] // NZ, N), ("z", "core", "ctx"))
    every = ("z", "core", "ctx")
    placed = (
        P(every, None),
        P(("z", "core")),
        P(),
        P(),
        P(None, "ctx"),
        P(None, "ctx"),
        P(None, "ctx"),
        P("ctx", None),
    )
    return jax.shard_map(on_device, mesh=split, in_specs=placed, out_specs=P(every, None), check_vma=False)
```

```python
import jax
import jax.numpy as jnp
from jax import lax
from jax.experimental import pallas as pl
from jax.experimental.pallas import tpu as pltpu
from jax.sharding import Mesh
from jax.sharding import PartitionSpec as P

HS = 128
HQ = 16
KVH = 4
CAP = 32
N = 16
TOK = 128
SEL = 256
D = 4096
SL = D // N
NP = 8
BF = jnp.bfloat16
F32 = jnp.float32
NT = (((1,), (1,)), ((), ()))
CHUNK = SEL + SEL // 2
PIECE = 16
VMEM = pltpu.VMEM


def one_hot(mask):
    return jnp.where(mask, 1.0, 0.0).astype(BF)


def slots(sel, me):
    base = me * TOK
    first = jnp.sum(jnp.where(sel < base, 1.0, 0.0), axis=1, keepdims=True).astype(jnp.int32)
    mine = (sel >= base) & (sel < base + TOK)
    rank = lax.broadcasted_iota(jnp.int32, (CAP, SEL), 1)
    slot = lax.broadcasted_iota(jnp.int32, (CAP, SEL), 0)
    by_slot = one_hot((rank - first == slot) & mine)
    token = lax.broadcasted_iota(jnp.int32, (TOK, SEL), 0)
    by_token = one_hot(token + base == sel)
    return by_slot, by_token


def column(row):
    same = lax.broadcasted_iota(jnp.int32, (SEL, SEL), 0) == lax.broadcasted_iota(jnp.int32, (SEL, SEL), 1)
    return jnp.sum(jnp.where(same, row.astype(F32), 0.0), axis=1, keepdims=True).astype(jnp.int32)


def pack_kernel(sel_ref, tok_hbm, gain_ref, wout_hbm, send_ref, tok_ref, wout_ref, sems):
    part, me = lax.axis_index(("z", "core")), lax.axis_index("ctx")
    parts = 4
    height = TOK // parts
    loads = [
        pltpu.make_async_copy(
            tok_hbm.at[pl.ds(i * height, height)], tok_ref.at[pl.ds(i * height, height)], sems.at[i]
        )
        for i in range(parts)
    ]
    loads.append(
        pltpu.make_async_copy(
            wout_hbm.at[pl.ds(pl.multiple_of(part * PIECE, PIECE), PIECE)], wout_ref, sems.at[parts]
        )
    )
    for load in loads:
        load.start()
    by_slot, by_token = slots(sel_ref[...], me)
    pick = lax.dot_general(by_slot, by_token, NT, preferred_element_type=F32).astype(BF)
    for load in loads:
        load.wait()
    raw = jnp.dot(pick, tok_ref[...], preferred_element_type=F32)
    scale = lax.rsqrt(jnp.mean(raw * raw, axis=1, keepdims=True) + 1e-05)
    normed = (raw * scale * gain_ref[...].reshape(1, D).astype(F32)).astype(BF)
    for c in range(N):
        for i in range(2):
            part = slice(c * SL + i * 128, c * SL + (i + 1) * 128)
            send_ref[c, i * CAP : (i + 1) * CAP, :] = normed[:, part]
            send_ref[c, 2 * CAP + i * PIECE : 2 * CAP + (i + 1) * PIECE, :] = wout_ref[:, part]


def compact_kernel(sel_ref, recv_ref, out_ref, piece_ref):
    sel_row = sel_ref[...]
    owner = column(sel_row) >> 7
    first = jnp.sum(jnp.where(sel_row < owner * TOK, 1.0, 0.0), axis=1, keepdims=True).astype(jnp.int32)
    place = owner * CAP + lax.broadcasted_iota(jnp.int32, (SEL, 1), 0) - first
    pick = one_hot(lax.broadcasted_iota(jnp.int32, (SEL, N * CAP), 1) == place)
    left = jnp.dot(pick, recv_ref[:, :CAP, :].reshape(N * CAP, 128), preferred_element_type=F32)
    right = jnp.dot(pick, recv_ref[:, CAP : 2 * CAP, :].reshape(N * CAP, 128), preferred_element_type=F32)
    dense = jnp.concatenate([left, right], axis=1).astype(BF)
    for d in range(N):
        out_ref[d] = dense
        piece_ref[d * 2 * PIECE : (d + 1) * 2 * PIECE, :] = recv_ref[d, 2 * CAP :, :]


def qkv_kernel(x_ref, wq_ref, wk_ref, wv_ref, qcos_ref, qsin_ref, kcos_ref, ksin_ref, out_ref):
    q = jnp.zeros((SEL, HS), F32)
    kv = jnp.zeros((SEL, 64), F32)
    for f in range(N):
        part = slice(f * SL, (f + 1) * SL)
        q += jnp.dot(x_ref[f], wq_ref[part, :], preferred_element_type=F32)
        both = jnp.concatenate([wk_ref[:, part], wv_ref[:, part]], axis=0)
        kv += lax.dot_general(x_ref[f], both, NT, preferred_element_type=F32)
    lane = lax.broadcasted_iota(jnp.int32, (SEL, 128), 1)
    q_mate = jnp.where(lane % 2 == 0, pltpu.roll(q, 127, 1), pltpu.roll(q, 1, 1))
    q = (q * qcos_ref[...] + q_mate * qsin_ref[...]).astype(BF)
    kv = jnp.concatenate([kv, kv], axis=1)
    kv_mate = jnp.where(lane % 8 < 4, pltpu.roll(kv, 124, 1), pltpu.roll(kv, 4, 1))
    kv = (kv * kcos_ref[...] + kv_mate * ksin_ref[...]).astype(BF)
    to = lax.broadcasted_iota(jnp.int32, (64, 128), 0)
    frm = lax.broadcasted_iota(jnp.int32, (64, 128), 1)
    order = one_hot(frm == ((to >> 3) & 1) * 32 + (to & 7) * 4 + (to >> 4))
    turned = lax.dot_general(order, kv, NT, preferred_element_type=F32).astype(BF)
    for d in range(N):
        out_ref[d, :SEL, :] = q
        out_ref[d, SEL : SEL + 64, :] = turned[:, :128]
        out_ref[d, SEL + 64 :, :] = turned[:, 128:]


def attend_kernel(sel_ref, recv_ref, wout_hbm, out_ref, wout_ref, mixed_ref, sems):
    parts = 4
    height = NP * N * 2 * PIECE // parts
    loads = [
        pltpu.make_async_copy(
            wout_hbm.at[pl.ds(i * height, height)], wout_ref.at[pl.ds(i * height, height)], sems.at[i]
        )
        for i in range(parts)
    ]
    for load in loads:
        load.start()
    left = recv_ref[:, SEL : SEL + 64, :].astype(F32).reshape(N, KVH, 2, 8, 128)
    right = recv_ref[:, SEL + 64 :, :].astype(F32).reshape(N, KVH, 2, 8, 128)
    causal = lax.broadcasted_iota(jnp.int32, (SEL, SEL), 0) >= lax.broadcasted_iota(jnp.int32, (SEL, SEL), 1)
    for g in range(KVH):
        keys, values = [
            jnp.concatenate([half[:, g, i].reshape(HS, 128) for half in (left, right)], axis=1).astype(BF)
            for i in range(2)
        ]
        for h in range(g * HQ // KVH, (g + 1) * HQ // KVH):
            scores = jnp.dot(recv_ref[h, :SEL, :], keys, preferred_element_type=F32) * (HS**-0.5)
            scores = jnp.where(causal, scores, -1e30)
            weights = jnp.exp(scores - jnp.max(scores, axis=1, keepdims=True))
            probs = (weights / jnp.sum(weights, axis=1, keepdims=True)).astype(BF)
            mixed = lax.dot_general(probs, values, NT, preferred_element_type=F32)
            mixed_ref[:, h * HS : (h + 1) * HS] = mixed.astype(BF)
    for load in loads:
        load.wait()
    update = jnp.zeros((SEL, SL), F32)
    for h in range(HQ):
        rows = [
            jnp.concatenate(
                [wout_ref[pl.ds(((m * N + h) * 2 + i) * PIECE, PIECE), :] for i in range(2)], axis=1
            )
            for m in range(NP)
        ]
        update += jnp.dot(
            mixed_ref[:, h * HS : (h + 1) * HS], jnp.concatenate(rows, axis=0), preferred_element_type=F32
        )
    sel_row = sel_ref[...]
    owner = sel_row >> 7
    first = jnp.sum(
        jnp.where(column(sel_row) < owner * TOK, 1.0, 0.0), axis=0, keepdims=True
    ).astype(jnp.int32)
    place = owner * CAP + lax.broadcasted_iota(jnp.int32, (1, SEL), 1) - first
    put = one_hot(lax.broadcasted_iota(jnp.int32, (N * CAP, SEL), 0) == place)
    sent = jnp.dot(put, update.astype(BF), preferred_element_type=F32).astype(BF)
    out_ref[...] = sent.reshape(N, CAP, SL)


def finish_kernel(sel_ref, tok_ref, router_ref, recv_ref, out_ref):
    by_slot, by_token = slots(sel_ref[...], lax.axis_index("ctx"))
    put = lax.dot_general(by_token, by_slot, NT, preferred_element_type=F32).astype(BF)
    live = jnp.sum(by_token.astype(F32), axis=1, keepdims=True) > 0.5
    router = router_ref[...].reshape(1, D).astype(F32)
    logit = jnp.sum(tok_ref[...].astype(F32) * router, axis=1, keepdims=True)
    gate = 1.0 / (1.0 + jnp.exp(-logit))
    for c in range(N):
        part = slice(c * SL, (c + 1) * SL)
        placed = jnp.dot(put, recv_ref[c], preferred_element_type=F32)
        old = tok_ref[:, part]
        fresh = (old.astype(F32) + gate * placed).astype(BF)
        out_ref[:, part] = jnp.where(live, fresh, old)


def call(kernel, name, shapes, in_hbm, flops, moved, scratch=()):
    return pl.pallas_call(
        kernel,
        out_shape=shapes,
        in_specs=[pl.BlockSpec(memory_space=pl.ANY if hbm else VMEM) for hbm in in_hbm],
        out_specs=jax.tree.map(lambda _: pl.BlockSpec(memory_space=VMEM), shapes),
        scratch_shapes=scratch,
        compiler_params=pltpu.CompilerParams(vmem_limit_bytes=40 * 1024 * 1024),
        cost_estimate=pl.CostEstimate(flops=flops, bytes_accessed=moved, transcendentals=0),
        name=name,
    )


def on_device(tokens, selected, norm_gain, router, w_query, w_key, w_value, w_out):
    me = lax.axis_index("ctx")
    shape = jax.ShapeDtypeStruct
    sel = selected.reshape(1, SEL)
    lane = jnp.arange(HS)
    position = selected.astype(F32)[:, None]

    def turn(component, used):
        pair = (component // 2).astype(F32)
        inverse = jnp.exp(-(2.0 * pair / HS) * jnp.log(10000.0))
        angle = position * jnp.where(used, inverse, 0.0)[None, :]
        return jnp.cos(angle), jnp.sin(angle) * jnp.where(component % 2 == 0, -1.0, 1.0)[None, :]

    q_cos, q_sin = turn(lane, lane < HS)
    k_cos, k_sin = turn(me * 8 + lane // 4, lane < 32)
    send = call(
        pack_kernel, "pack", shape((N, 2 * CAP + 2 * PIECE, 128), BF), (0, 1, 0, 1), 2 * CAP * TOK * D, 2 << 20,
        [VMEM((TOK, D), BF), VMEM((PIECE, D), BF), pltpu.SemaphoreType.DMA((5,))],
    )(sel, tokens, norm_gain, w_out)
    got = lax.all_to_all(send, "ctx", 0, 0, tiled=True)
    copies, piece = call(
        compact_kernel, "compact", (shape((N, SEL, SL), BF), shape((N * 2 * PIECE, 128), BF)), (0, 0),
        2 * SEL * 512 * SL, 3 << 20,
    )(sel, got)
    w_slice = lax.all_gather(piece, ("z", "core"), axis=0, tiled=True)
    rows = lax.all_to_all(copies, "ctx", 0, 0, tiled=True)
    qkv = call(qkv_kernel, "qkv", shape((N, CHUNK, HS), BF), (0,) * 8, 2 * SEL * D * 256, 6 << 20)(
        rows, w_query, w_key.T, w_value.T, q_cos, q_sin, k_cos, k_sin
    )
    heads = lax.all_to_all(qkv, "ctx", 0, 0, tiled=True)
    update = call(
        attend_kernel, "attend", shape((N, CAP, SL), BF), (0, 0, 1), 2 * 16 * 3 * 256 * 256 * 128, 4 << 20,
        [VMEM((NP * N * 2 * PIECE, 128), BF), VMEM((SEL, HQ * HS), BF), pltpu.SemaphoreType.DMA((4,))],
    )(sel, heads, w_slice)
    back = lax.all_to_all(update, "ctx", 0, 0, tiled=True)
    return call(finish_kernel, "finish", shape((TOK, D), BF), (0,) * 4, 2 * TOK * CAP * D, 4 << 20)(
        sel, tokens, router, back
    )


def solution(mesh):
    split = Mesh(mesh.devices.reshape(-1, 4, 2, N), ("block", "z", "core", "ctx"))
    every = ("block", "z", "core", "ctx")
    placed = (
        P(every, None),
        P(("block", "z", "core")),
        P(),
        P(),
        P(None, "ctx"),
        P(None, "ctx"),
        P(None, "ctx"),
        P("ctx", None),
    )
    return jax.shard_map(on_device, mesh=split, in_specs=placed, out_specs=P(every, None), check_vma=False)
```

```python
import jax
import jax.numpy as jnp
from jax import lax
from jax.experimental import pallas as pl
from jax.experimental.pallas import tpu as pltpu
from jax.sharding import Mesh
from jax.sharding import PartitionSpec as P

HS = 128
HQ = 16
KVH = 4
CAP = 32
N = 16
G = 4
TOK = 128
SEL = 256
D = 4096
Q = D // G
H = Q // 2
BF = jnp.bfloat16
F32 = jnp.float32
NT = (((1,), (1,)), ((), ()))
CHUNK = SEL + SEL // 2
VMEM = pltpu.VMEM


def one_hot(mask):
    return jnp.where(mask, 1.0, 0.0).astype(BF)


def iota(shape, axis):
    return lax.broadcasted_iota(jnp.int32, shape, axis)


def slots(sel, me):
    base = me * TOK
    first = jnp.sum(jnp.where(sel < base, 1.0, 0.0), axis=1, keepdims=True).astype(jnp.int32)
    mine = (sel >= base) & (sel < base + TOK)
    by_slot = one_hot((iota((CAP, SEL), 1) - first == iota((CAP, SEL), 0)) & mine)
    by_token = one_hot(iota((TOK, SEL), 0) + base == sel)
    return by_slot, by_token


def column(row):
    same = iota((SEL, SEL), 0) == iota((SEL, SEL), 1)
    return jnp.sum(jnp.where(same, row.astype(F32), 0.0), axis=1, keepdims=True).astype(jnp.int32)


def pack_kernel(sel_ref, gain_ref, tok_hbm, wq_hbm, wk_hbm, wv_hbm, send_ref, tok_ref, sems):
    me, core = lax.axis_index(("x", "y")), lax.axis_index("core")
    loads = []

    def load(source, target):
        loads.append(pltpu.make_async_copy(source, target, sems.at[len(loads)]))
        loads[-1].start()

    for i in range(4):
        load(tok_hbm.at[pl.ds(i * 32, 32)], tok_ref.at[pl.ds(i * 32, 32)])
    for t in range(G):
        start = pl.multiple_of(t * Q + core * H, H)
        for i in range(4):
            load(wq_hbm.at[pl.ds(start + i * 128, 128)], send_ref.at[t, pl.ds(0, 128), pl.ds(i * 128, 128)])
        load(wk_hbm.at[:, pl.ds(start, H)], send_ref.at[t, pl.ds(128, 32)])
        load(wv_hbm.at[:, pl.ds(start, H)], send_ref.at[t, pl.ds(160, 32)])
    by_slot, by_token = slots(sel_ref[...], me)
    pick = lax.dot_general(by_slot, by_token, NT, preferred_element_type=F32).astype(BF)
    for copy in loads[:4]:
        copy.wait()
    raw = jnp.dot(pick, tok_ref[...], preferred_element_type=F32)
    scale = lax.rsqrt(jnp.mean(raw * raw, axis=1, keepdims=True) + 1e-05)
    normed = (raw * scale * gain_ref[...].reshape(1, D).astype(F32)).astype(BF)
    for t in range(G):
        send_ref[t, 192:224, :] = normed[:, t * Q : t * Q + H]
        send_ref[t, 224:256, :] = normed[:, t * Q + H : (t + 1) * Q]
    for copy in loads[4:]:
        copy.wait()


def spread_kernel(got_ref, wout_hbm, send_ref, sems):
    core = lax.axis_index("core")
    loads = []
    for t in range(G):
        for i in range(2):
            loads.append(
                pltpu.make_async_copy(
                    wout_hbm.at[pl.ds(pl.multiple_of(core * 64, 64), 64), pl.ds(t * Q + i * H, H)],
                    send_ref.at[t, pl.ds(256 + i * 64, 64)],
                    sems.at[len(loads)],
                )
            )
            loads[-1].start()
    for s in range(G):
        rows = got_ref[s, 192:256, :]
        for t in range(G):
            send_ref[t, s * 64 : (s + 1) * 64, :] = rows
    for copy in loads:
        copy.wait()


def project_kernel(sel_ref, rows_ref, own_ref, other_ref, send_ref, wout_ref, x_ref):
    core = lax.axis_index("core")
    sel_row = sel_ref[...]
    owner = column(sel_row) >> 7
    first = jnp.sum(jnp.where(sel_row < owner * TOK, 1.0, 0.0), axis=1, keepdims=True).astype(jnp.int32)
    place = ((owner & 3) * G + (owner >> 2)) * CAP + iota((SEL, 1), 0) - first
    pick = one_hot(iota((SEL, N * CAP), 1) == place)
    for i in range(2):
        padded = jnp.concatenate(
            [rows_ref[s, t * 64 + i * 32 : t * 64 + (i + 1) * 32, :] for s in range(G) for t in range(G)], axis=0
        )
        x_ref[i] = jnp.dot(pick, padded, preferred_element_type=F32).astype(BF)
    q = jnp.zeros((SEL, G * HS), F32)
    kv = jnp.zeros((SEL, G * 64), F32)
    for w_ref, i in ((own_ref, core), (other_ref, 1 - core)):
        w_q = jnp.concatenate(
            [
                jnp.concatenate([w_ref[s, :128, b * 128 : (b + 1) * 128] for b in range(4)], axis=0)
                for s in range(G)
            ],
            axis=1,
        )
        w_kv = jnp.concatenate([w_ref[s, 128:192, :] for s in range(G)], axis=0)
        q += jnp.dot(x_ref[i], w_q, preferred_element_type=F32)
        kv += lax.dot_general(x_ref[i], w_kv, NT, preferred_element_type=F32)
    to, frm = iota((SEL, SEL), 0), iota((SEL, SEL), 1)
    order = one_hot(frm == ((to >> 4) & 3) * 64 + ((to >> 3) & 1) * 32 + (to & 7) * 4 + (to >> 6))
    turned = lax.dot_general(order, kv.astype(BF), NT, preferred_element_type=F32).astype(BF)
    for t in range(G):
        send_ref[t, :SEL, :] = q[:, t * HS : (t + 1) * HS].astype(BF)
        send_ref[t, SEL : SEL + 64, :] = turned[t * 64 : (t + 1) * 64, :128]
        send_ref[t, SEL + 64 :, :] = turned[t * 64 : (t + 1) * 64, 128:]
        wout_ref[t] = rows_ref[t, 256:, :]


def turn_kernel(parts_ref, q_cos_ref, q_sin_ref, k_cos_ref, k_sin_ref, send_ref):
    total = sum(parts_ref[s].astype(F32) for s in range(G))
    q = total[:SEL]
    mate = jnp.where(iota((SEL, HS), 1) % 2 == 0, pltpu.roll(q, HS - 1, 1), pltpu.roll(q, 1, 1))
    q = (q * q_cos_ref[...] + mate * q_sin_ref[...]).astype(BF)
    kv = jnp.concatenate([total[SEL : SEL + 64], total[SEL + 64 :]], axis=1)
    mate = jnp.where(iota((64, SEL), 0) % 2 == 0, pltpu.roll(kv, 63, 0), pltpu.roll(kv, 1, 0))
    kv = (kv * k_cos_ref[...] + mate * k_sin_ref[...]).astype(BF)
    for t in range(G):
        send_ref[t, :SEL, :] = q
        send_ref[t, SEL : SEL + 64, :] = kv[:, :128]
        send_ref[t, SEL + 64 :, :] = kv[:, 128:]


def attend_kernel(sel_ref, heads_ref, own_ref, other_ref, out_ref, mixed_ref):
    core = lax.axis_index("core")
    halves = [
        heads_ref[:, SEL + i * 64 : SEL + (i + 1) * 64, :].astype(F32).reshape(G, G, 2, 8, 128) for i in range(2)
    ]
    keys, values = [
        jnp.concatenate(
            [
                jnp.concatenate([half[y, x, i] for x in range(G) for y in range(G)], axis=0).astype(BF)
                for half in halves
            ],
            axis=1,
        )
        for i in range(2)
    ]
    causal = iota((SEL, SEL), 0) >= iota((SEL, SEL), 1)
    for h in range(G):
        scores = jnp.dot(heads_ref[h, :SEL, :], keys, preferred_element_type=F32) * (HS**-0.5)
        scores = jnp.where(causal, scores, -1e30)
        weights = jnp.exp(scores - jnp.max(scores, axis=1, keepdims=True))
        probs = (weights / jnp.sum(weights, axis=1, keepdims=True)).astype(BF)
        mixed = lax.dot_general(probs, values, NT, preferred_element_type=F32)
        mixed_ref[:, h * HS : (h + 1) * HS] = mixed.astype(BF)
    sel_row = sel_ref[...]
    owner = sel_row >> 7
    first = jnp.sum(
        jnp.where(column(sel_row) < owner * TOK, 1.0, 0.0), axis=0, keepdims=True
    ).astype(jnp.int32)
    place = owner * CAP + iota((1, SEL), 1) - first
    put = one_hot(iota((N * CAP, SEL), 0) == place)
    for i in range(2):
        rows = []
        for h in range(G):
            own, other = own_ref[h, i * 64 : (i + 1) * 64, :], other_ref[h, i * 64 : (i + 1) * 64, :]
            rows += [jnp.where(core == 0, own, other), jnp.where(core == 0, other, own)]
        update = jnp.dot(mixed_ref[...], jnp.concatenate(rows, axis=0), preferred_element_type=F32).astype(BF)
        sent = jnp.dot(put, update, preferred_element_type=F32).astype(BF)
        out_ref[:, :, i * H : (i + 1) * H] = sent.reshape(N, CAP, H)


def finish_kernel(sel_ref, tok_ref, router_ref, parts_ref, out_ref):
    by_slot, by_token = slots(sel_ref[...], lax.axis_index(("x", "y")))
    put = lax.dot_general(by_token, by_slot, NT, preferred_element_type=F32).astype(BF)
    put = jnp.concatenate([put] * G, axis=1)
    live = jnp.sum(by_token.astype(F32), axis=1, keepdims=True) > 0.5
    router = router_ref[...].reshape(1, D).astype(F32)
    logit = jnp.sum(tok_ref[...].astype(F32) * router, axis=1, keepdims=True)
    gate = 1.0 / (1.0 + jnp.exp(-logit))
    for y in range(G):
        terms = jnp.concatenate([parts_ref[x * G + y] for x in range(G)], axis=0)
        placed = jnp.dot(put, terms, preferred_element_type=F32)
        part = slice(y * Q, (y + 1) * Q)
        old = tok_ref[:, part]
        fresh = (old.astype(F32) + gate * placed).astype(BF)
        out_ref[:, part] = jnp.where(live, fresh, old)


def call(kernel, name, shapes, in_hbm, flops, moved, scratch=()):
    return pl.pallas_call(
        kernel,
        out_shape=shapes,
        in_specs=[pl.BlockSpec(memory_space=pl.ANY if hbm else VMEM) for hbm in in_hbm],
        out_specs=jax.tree.map(lambda _: pl.BlockSpec(memory_space=VMEM), shapes),
        scratch_shapes=scratch,
        compiler_params=pltpu.CompilerParams(vmem_limit_bytes=40 * 1024 * 1024),
        cost_estimate=pl.CostEstimate(flops=flops, bytes_accessed=moved, transcendentals=0),
        name=name,
    )


def on_device(tokens, selected, norm_gain, router, w_query, w_key, w_value, w_out):
    y = lax.axis_index("y")
    shape = jax.ShapeDtypeStruct
    dma = pltpu.SemaphoreType.DMA
    sel = selected.reshape(1, SEL)
    position = selected.astype(F32)

    def turn(component, used):
        pair = (component // 2).astype(F32)
        inverse = jnp.exp(-(2.0 * pair / HS) * jnp.log(10000.0))
        return jnp.where(used, inverse, 0.0), jnp.where(component % 2 == 0, -1.0, 1.0)

    lane = jnp.arange(HS)
    inverse, sign = turn(lane, True)
    angle = position[:, None] * inverse[None, :]
    q_cos, q_sin = jnp.cos(angle), jnp.sin(angle) * sign[None, :]
    row = jnp.arange(64)
    inverse, sign = turn(8 * (G * (row // 16) + y) + row % 8, row % 16 < 8)
    angle = inverse[:, None] * position[None, :]
    k_cos, k_sin = jnp.cos(angle), jnp.sin(angle) * sign[:, None]

    def swap(half):
        return lax.ppermute(half, "core", [(0, 1), (1, 0)])

    send = call(
        pack_kernel, "pack", shape((G, 256, H), BF), (0, 0, 1, 1, 1, 1), 2 * CAP * TOK * D, 2 << 20,
        [VMEM((TOK, D), BF), dma((4 + 6 * G,))],
    )(sel, norm_gain, tokens, w_query, w_key.T, w_value.T)
    own = lax.all_to_all(send, "x", 0, 0, tiled=True)
    other = swap(own)
    send = call(
        spread_kernel, "spread", shape((G, 384, H), BF), (0, 1), 1 << 20, 3 << 20, [dma((2 * G,))]
    )(own, w_out)
    rows = lax.all_to_all(send, "y", 0, 0, tiled=True)
    send, w_own = call(
        project_kernel, "project", (shape((G, CHUNK, HS), BF), shape((G, 128, H), BF)), (0,) * 4,
        2 * SEL * Q * 1280, 5 << 20, [VMEM((2, SEL, H), BF)],
    )(sel, rows, own, other)
    w_other = swap(w_own)
    parts = lax.all_to_all(send, "x", 0, 0, tiled=True)
    send = call(turn_kernel, "turn", shape((G, CHUNK, HS), BF), (0,) * 5, SEL * HS * 20, 1 << 20)(
        parts, q_cos, q_sin, k_cos, k_sin
    )
    heads = lax.all_to_all(send, "y", 0, 0, tiled=True)
    send = call(
        attend_kernel, "attend", shape((N, CAP, Q), BF), (0,) * 4, 2 * SEL * 1024 * 1300, 4 << 20,
        [VMEM((SEL, G * HS), BF)],
    )(sel, heads, w_own, w_other)
    parts = lax.all_to_all(send, ("x", "y"), 0, 0, tiled=True)
    return call(finish_kernel, "finish", shape((TOK, D), BF), (0,) * 4, 2 * TOK * TOK * D, 4 << 20)(
        sel, tokens, router, parts
    )


def solution(mesh):
    split = Mesh(mesh.devices.reshape(-1, 2, G, G), ("z", "core", "x", "y"))
    every = ("z", "core", "x", "y")
    across = P(None, ("x", "y"))
    placed = (P(every, None), P(("z", "core")), P(), P(), across, across, across, P(("x", "y"), None))
    return jax.shard_map(on_device, mesh=split, in_specs=placed, out_specs=P(every, None), check_vma=False)
```

```python
import jax
import jax.numpy as jnp
from jax import lax
from jax.experimental import pallas as pl
from jax.experimental.pallas import tpu as pltpu
from jax.sharding import Mesh
from jax.sharding import PartitionSpec as P

HS = 128
HQ = 16
KVH = 4
CAP = 32
N = 16
G = 4
TOK = 128
SEL = 256
D = 4096
Q = D // G
H = Q // 2
W = Q // 4
BF = jnp.bfloat16
F32 = jnp.float32
NT = (((1,), (1,)), ((), ()))
CHUNK = SEL + SEL // 2
VMEM = pltpu.VMEM


def one_hot(mask):
    return jnp.where(mask, 1.0, 0.0).astype(BF)


def iota(shape, axis):
    return lax.broadcasted_iota(jnp.int32, shape, axis)


def slots(sel, me):
    base = me * TOK
    first = jnp.sum(jnp.where(sel < base, 1.0, 0.0), axis=1, keepdims=True).astype(jnp.int32)
    mine = (sel >= base) & (sel < base + TOK)
    by_slot = one_hot((iota((CAP, SEL), 1) - first == iota((CAP, SEL), 0)) & mine)
    by_token = one_hot(iota((TOK, SEL), 0) + base == sel)
    return by_slot, by_token


def column(row):
    same = iota((SEL, SEL), 0) == iota((SEL, SEL), 1)
    return jnp.sum(jnp.where(same, row.astype(F32), 0.0), axis=1, keepdims=True).astype(jnp.int32)


def quarter():
    return 2 * lax.axis_index("core") + lax.axis_index("z") % 2


def pack_kernel(sel_hbm, gain_hbm, tok_hbm, wq_hbm, wk_hbm, wv_hbm, send_ref, sel_ref, gain_ref, tok_ref, sems):
    me, mine = lax.axis_index(("x", "y")), quarter()
    loads = []

    def load(source, target):
        loads.append(pltpu.make_async_copy(source, target, sems.at[len(loads)]))
        loads[-1].start()

    load(sel_hbm, sel_ref)
    for i in range(4):
        load(tok_hbm.at[pl.ds(i * 32, 32)], tok_ref.at[pl.ds(i * 32, 32)])
    load(gain_hbm, gain_ref)
    for t in range(G):
        start = pl.multiple_of(t * Q + mine * W, W)
        for i in range(4):
            load(wq_hbm.at[pl.ds(start + i * 64, 64)], send_ref.at[t, pl.ds(0, 64), pl.ds(i * 128, 128)])
        load(wk_hbm.at[:, pl.ds(start, W)], send_ref.at[t, pl.ds(64, 32), pl.ds(0, W)])
        load(wv_hbm.at[:, pl.ds(start, W)], send_ref.at[t, pl.ds(64, 32), pl.ds(W, W)])
    loads[0].wait()
    by_slot, by_token = slots(sel_ref[...], me)
    pick = lax.dot_general(by_slot, by_token, NT, preferred_element_type=F32).astype(BF)
    for copy in loads[1:6]:
        copy.wait()
    raw = jnp.dot(pick, tok_ref[...], preferred_element_type=F32)
    scale = lax.rsqrt(jnp.mean(raw * raw, axis=1, keepdims=True) + 1e-05)
    normed = (raw * scale * gain_ref[...].reshape(1, D).astype(F32)).astype(BF)
    for t in range(G):
        send_ref[t, 96:128, :] = normed[:, t * Q : t * Q + H]
        send_ref[t, 128:160, :] = normed[:, t * Q + H : (t + 1) * Q]
    for copy in loads[6:]:
        copy.wait()


def spread_kernel(got_ref, wout_hbm, send_ref, weight_ref, sems):
    core = lax.axis_index("core")
    loads = []
    for t in range(G):
        for i in range(2):
            loads.append(
                pltpu.make_async_copy(
                    wout_hbm.at[pl.ds(pl.multiple_of(core * 64, 64), 64), pl.ds(t * Q + i * H, H)],
                    send_ref.at[t, pl.ds(256 + i * 64, 64)],
                    sems.at[len(loads)],
                )
            )
            loads[-1].start()
    for s in range(G):
        rows = got_ref[s, 96:160, :]
        for t in range(G):
            send_ref[t, s * 64 : (s + 1) * 64, :] = rows
        weight_ref[s] = got_ref[s, :96, :]
    for copy in loads:
        copy.wait()


def project_kernel(sel_ref, rows_ref, w0_ref, w1_ref, w2_ref, w3_ref, send_ref, wout_ref, x_ref):
    mine = quarter()
    sel_row = sel_ref[...]
    owner = column(sel_row) >> 7
    first = jnp.sum(jnp.where(sel_row < owner * TOK, 1.0, 0.0), axis=1, keepdims=True).astype(jnp.int32)
    place = ((owner & 3) * G + (owner >> 2)) * CAP + iota((SEL, 1), 0) - first
    pick = one_hot(iota((SEL, N * CAP), 1) == place)
    for i in range(2):
        padded = jnp.concatenate(
            [rows_ref[s, t * 64 + i * 32 : t * 64 + (i + 1) * 32, :] for s in range(G) for t in range(G)], axis=0
        )
        dense = jnp.dot(pick, padded, preferred_element_type=F32).astype(BF)
        x_ref[2 * i], x_ref[2 * i + 1] = dense[:, :W], dense[:, W:]
    q = jnp.zeros((SEL, G * HS), F32)
    kv = jnp.zeros((SEL, G * 64), F32)
    for i, w_ref in enumerate((w0_ref, w1_ref, w2_ref, w3_ref)):
        x = x_ref[mine ^ i]
        w_q = jnp.concatenate(
            [
                jnp.concatenate([w_ref[s, :64, b * 128 : (b + 1) * 128] for b in range(4)], axis=0)
                for s in range(G)
            ],
            axis=1,
        )
        w_kv = jnp.concatenate([w_ref[s, 64:96, b * W : (b + 1) * W] for s in range(G) for b in range(2)], axis=0)
        q += jnp.dot(x, w_q, preferred_element_type=F32)
        kv += lax.dot_general(x, w_kv, NT, preferred_element_type=F32)
    to, frm = iota((SEL, SEL), 0), iota((SEL, SEL), 1)
    order = one_hot(frm == ((to >> 4) & 3) * 64 + ((to >> 3) & 1) * 32 + (to & 7) * 4 + (to >> 6))
    turned = lax.dot_general(order, kv.astype(BF), NT, preferred_element_type=F32).astype(BF)
    for t in range(G):
        send_ref[t, :SEL, :] = q[:, t * HS : (t + 1) * HS].astype(BF)
        send_ref[t, SEL : SEL + 64, :] = turned[t * 64 : (t + 1) * 64, :128]
        send_ref[t, SEL + 64 :, :] = turned[t * 64 : (t + 1) * 64, 128:]
        wout_ref[t] = rows_ref[t, 256:, :]


def turn_kernel(parts_ref, table_ref, send_ref):
    total = sum(parts_ref[s].astype(F32) for s in range(G))
    q = total[:SEL]
    mate = jnp.where(iota((SEL, HS), 1) % 2 == 0, pltpu.roll(q, HS - 1, 1), pltpu.roll(q, 1, 1))
    q = (q * table_ref[:SEL, :HS] + mate * table_ref[:SEL, HS:]).astype(BF)
    kv = jnp.concatenate([total[SEL : SEL + 64], total[SEL + 64 :]], axis=1)
    mate = jnp.where(iota((64, SEL), 0) % 2 == 0, pltpu.roll(kv, 63, 0), pltpu.roll(kv, 1, 0))
    kv = (kv * table_ref[SEL : SEL + 64] + mate * table_ref[SEL + 64 :]).astype(BF)
    for t in range(G):
        send_ref[t, :SEL, :] = q
        send_ref[t, SEL : SEL + 64, :] = kv[:, :128]
        send_ref[t, SEL + 64 :, :] = kv[:, 128:]


def attend_kernel(sel_ref, heads_ref, near_ref, far_ref, out_ref, mixed_ref, wout_ref):
    core = lax.axis_index("core")
    for i, w_ref in ((core, near_ref), (1 - core, far_ref)):
        for h in range(G):
            wout_ref[h, i] = jnp.concatenate([w_ref[h, :64, :], w_ref[h, 64:, :]], axis=1)
    halves = [
        heads_ref[:, SEL + i * 64 : SEL + (i + 1) * 64, :].astype(F32).reshape(G, G, 2, 8, 128) for i in range(2)
    ]
    keys, values = [
        jnp.concatenate(
            [
                jnp.concatenate([half[y, x, i] for x in range(G) for y in range(G)], axis=0).astype(BF)
                for half in halves
            ],
            axis=1,
        )
        for i in range(2)
    ]
    causal = iota((SEL, SEL), 0) >= iota((SEL, SEL), 1)
    for h in range(G):
        scores = jnp.dot(heads_ref[h, :SEL, :], keys, preferred_element_type=F32) * (HS**-0.5)
        scores = jnp.where(causal, scores, -1e30)
        weights = jnp.exp(scores - jnp.max(scores, axis=1, keepdims=True))
        probs = (weights / jnp.sum(weights, axis=1, keepdims=True)).astype(BF)
        mixed = lax.dot_general(probs, values, NT, preferred_element_type=F32)
        mixed_ref[:, h * HS : (h + 1) * HS] = mixed.astype(BF)
    sel_row = sel_ref[...]
    owner = sel_row >> 7
    first = jnp.sum(
        jnp.where(column(sel_row) < owner * TOK, 1.0, 0.0), axis=0, keepdims=True
    ).astype(jnp.int32)
    place = owner * CAP + iota((1, SEL), 1) - first
    put = one_hot(iota((N * CAP, SEL), 0) == place)
    update = jnp.dot(mixed_ref[...], wout_ref[...].reshape(G * HS, Q), preferred_element_type=F32).astype(BF)
    sent = jnp.dot(put, update, preferred_element_type=F32).astype(BF)
    out_ref[...] = sent.reshape(N, CAP, Q)


def gate_kernel(sel_ref, tok_ref, router_ref, gate_ref, put_ref):
    by_slot, by_token = slots(sel_ref[...], lax.axis_index(("x", "y")))
    put = lax.dot_general(by_token, by_slot, NT, preferred_element_type=F32).astype(BF)
    put_ref[...] = jnp.concatenate([put] * G, axis=1)
    router = router_ref[...].reshape(1, D).astype(F32)
    logit = jnp.sum(tok_ref[...].astype(F32) * router, axis=1, keepdims=True)
    gate_ref[...] = jnp.broadcast_to(1.0 / (1.0 + jnp.exp(-logit)), (TOK, 128))


def finish_kernel(tok_ref, gate_ref, put_ref, parts_ref, out_hbm, out_ref, sems):
    gate = gate_ref[:, :1]
    stores = []
    for y in range(G):
        terms = jnp.concatenate([parts_ref[x * G + y] for x in range(G)], axis=0)
        placed = jnp.dot(put_ref[...], terms, preferred_element_type=F32)
        part = slice(y * Q, (y + 1) * Q)
        out_ref[:, part] = (tok_ref[:, part].astype(F32) + gate * placed).astype(BF)
        there = pl.ds(y * Q, Q)
        stores.append(pltpu.make_async_copy(out_ref.at[:, there], out_hbm.at[:, there], sems.at[y]))
        stores[-1].start()
    for store in stores:
        store.wait()


def call(kernel, name, shapes, spaces, flops, moved, scratch=(), out=VMEM, vmem=40):
    where = {"v": VMEM, "h": pltpu.HBM, "a": pl.ANY}
    return pl.pallas_call(
        kernel,
        out_shape=shapes,
        in_specs=[pl.BlockSpec(memory_space=where[space]) for space in spaces],
        out_specs=jax.tree.map(lambda _: pl.BlockSpec(memory_space=out), shapes),
        scratch_shapes=scratch,
        compiler_params=pltpu.CompilerParams(vmem_limit_bytes=vmem * 1024 * 1024),
        cost_estimate=pl.CostEstimate(flops=flops, bytes_accessed=moved, transcendentals=0),
        name=name,
    )


def on_device(tokens, selected, norm_gain, router, w_query, w_key, w_value, w_out):
    y = lax.axis_index("y")
    shape = jax.ShapeDtypeStruct
    dma = pltpu.SemaphoreType.DMA
    sel = selected.reshape(1, SEL)
    def complete(piece, before=()):
        size = lax.axis_size("z")
        pairs = [(z, z ^ 1) for z in range(size)]
        near = lax.ppermute(piece, "z", pairs)
        cores = [(0, 1), (1, 0)]
        piece, before = lax.optimization_barrier((piece, before))
        return (piece, near, lax.ppermute(piece, "core", cores), lax.ppermute(near, "core", cores)), before

    send = call(
        pack_kernel, "pack", shape((G, 160, H), BF), "hhhhhh", 2 * CAP * TOK * D, 2 << 20,
        [VMEM((1, SEL), jnp.int32), VMEM((D,), BF), VMEM((TOK, D), BF), dma((6 + 6 * G,))], vmem=40,
    )(*[pltpu.with_memory_space_constraint(v, pltpu.HBM) for v in (sel, norm_gain, tokens, w_query, w_key.T, w_value.T)])
    got = lax.all_to_all(send, "x", 0, 0, tiled=True)
    send, piece = call(
        spread_kernel, "spread", (shape((G, 384, H), BF), shape((G, 96, H), BF)), "vh", 1 << 20, 3 << 20,
        [dma((2 * G,))],
    )(got, w_out)
    late, tokens_late, router, piece = lax.optimization_barrier((selected, tokens, router, piece))
    position = late.astype(F32)

    def turn(component, used):
        pair = (component // 2).astype(F32)
        inverse = jnp.exp(-(2.0 * pair / HS) * jnp.log(10000.0))
        return jnp.where(used, inverse, 0.0), jnp.where(component % 2 == 0, -1.0, 1.0)

    lane = jnp.arange(HS)
    inverse, sign = turn(lane, True)
    angle = position[:, None] * inverse[None, :]
    q_cos, q_sin = jnp.cos(angle), jnp.sin(angle) * sign[None, :]
    row = jnp.arange(64)
    inverse, sign = turn(8 * (G * (row // 16) + y) + row % 8, row % 16 < 8)
    angle = inverse[:, None] * position[None, :]
    k_cos, k_sin = jnp.cos(angle), jnp.sin(angle) * sign[:, None]
    table = jnp.concatenate([jnp.concatenate([q_cos, q_sin], axis=1), k_cos, k_sin], axis=0)
    gate, put = call(
        gate_kernel, "gate", (shape((TOK, 128), F32), shape((TOK, TOK), BF)), "vvv", TOK * D * 2, 2 << 20
    )(late.reshape(1, SEL), tokens_late, router)
    weights, (gate, put, table) = complete(piece, (gate, put, table))
    rows = lax.all_to_all(send, "y", 0, 0, tiled=True)
    rows, gate, put, table = lax.optimization_barrier((rows, gate, put, table))
    send, piece = call(
        project_kernel, "project", (shape((G, CHUNK, HS), BF), shape((G, 128, H), BF)), "vvvvvv",
        2 * SEL * Q * 1280, 5 << 20, [VMEM((4, SEL, W), BF)],
    )(sel, rows, *weights)
    w_near, w_far = piece, lax.ppermute(piece, "core", [(0, 1), (1, 0)])
    parts = lax.all_to_all(send, "x", 0, 0, tiled=True)
    send = call(turn_kernel, "turn", shape((G, CHUNK, HS), BF), "vv", SEL * HS * 20, 1 << 20)(parts, table)
    heads = lax.all_to_all(send, "y", 0, 0, tiled=True)
    send = call(
        attend_kernel, "attend", shape((N, CAP, Q), BF), "vvvv", 2 * SEL * 1024 * 1300, 4 << 20,
        [VMEM((SEL, G * HS), BF), VMEM((G, 2, 64, Q), BF)],
    )(sel, heads, w_near, w_far)
    parts = lax.all_to_all(send, ("x", "y"), 0, 0, tiled=True)
    return call(
        finish_kernel, "finish", shape((TOK, D), BF), "vvvv", 2 * TOK * TOK * D, 4 << 20,
        [VMEM((TOK, D), BF), dma((G,))], pltpu.HBM,
    )(tokens, gate, put, parts)


def solution(mesh):
    split = Mesh(mesh.devices.reshape(-1, 2, G, G), ("z", "core", "x", "y"))
    every = ("z", "core", "x", "y")
    across = P(None, ("x", "y"))
    placed = (P(every, None), P(("z", "core")), P(), P(), across, across, across, P(("x", "y"), None))
    return jax.shard_map(on_device, mesh=split, in_specs=placed, out_specs=P(every, None), check_vma=False)
```
